32 devices in a mesh: row: 8 (over z, x), col: 4 (over y, core).
Axes of the slice: x: 2, y: 2, z: 4, core: 2. Of those that a mesh axis runs over, the one named last changes fastest.
Arguments:
- vectors: float32 [64, 4096], P(None, ('row', 'col')), may hold values from -6 to 6
- blocks: bfloat16 [8, 4, 152, 128, 128], P('row', 'col'), may hold values from -0.0390625 to 0.0390625
- slot_block_rows: int32 [8, 4, 152], P('row', 'col'), may hold values from 0 to 3
- slot_block_columns: int32 [8, 4, 152], P('row', 'col'), may hold values from 0 to 7
- counts: int32 [8, 4], P('row', 'col'), may hold values from 38 to 152, as said below
Outputs:
- filtered: float32 [64, 4096], P(None, ('row', 'col'))
The draws below stay inside these ranges and needn't reach their ends.
Inputs may be any that keep to these rules, and one draw needn't show every extreme that they name: `counts`: slots at or after a device's count carry no block.
All inputs are finite; a program needn't handle non-finite values.
Results may differ from the reference program's by a relative error of at most 0.023.
Values may be sent and summed in bfloat16 or wider, within the bound.
A program may use at most 64 MiB of HBM per device.

```python
import jax
import jax.numpy as jnp
from jax import lax

ORBITAL_COUNT = 128
K = 64
DEVICE_SLOTS = 152
DEGREE = 3
N = 4096
SLAB_BLOCK_ROWS = 4
SLAB_BLOCK_COLS = 8
NBLK = 32
N_ROW = 8
N_COL = 4


def draw_counts(key, part):
    key = jax.random.fold_in(key, 11)
    leading_entry, second = jax.random.split(key)
    start_offset = jax.random.randint(leading_entry, (N_ROW * N_COL,), DEVICE_SLOTS // 4, DEVICE_SLOTS + 1).astype(jnp.int32)
    busiest_device = jax.random.randint(second, (), 0, N_ROW * N_COL).astype(jnp.int32)
    slot_positions = jnp.arange(N_ROW * N_COL, dtype=jnp.int32)
    start_offset = jnp.where(slot_positions == busiest_device, jnp.int32(DEVICE_SLOTS), start_offset)
    return start_offset.reshape(N_ROW, N_COL)


def with_ends(array, key, least, largest):
    extent = array.shape
    spot = [jax.random.randint(jax.random.fold_in(key, axis), (), 0, extent[axis]) for axis in range(len(extent))]
    array = array.at[tuple(spot)].set(least)
    longest = extent.index(max(extent))
    spot[longest] = (spot[longest] + 1) % extent[longest]
    return array.at[tuple(spot)].set(largest)


def shard_levels(own_key, shape, pieces, low, high):
    gain = 1.0
    for position, blocks in pieces:
        heights = jax.random.uniform(jax.random.fold_in(jax.random.fold_in(own_key, 6), position), (blocks,), jnp.float32, low / len(pieces), high / len(pieces))
        gain = gain * jnp.repeat(jnp.exp(heights), shape[position] // blocks).reshape((-1,) + (1,) * (len(shape) - 1 - position))
    return gain


def centred(key, shape, scale, bound, cuts=(), kind=jnp.bfloat16):
    drawn = jax.random.normal(key, shape, jnp.float32) * scale
    if len(cuts) > 0:
        drawn = shard_levels(key, shape, cuts, -0.22, 0.18) * drawn
    return jnp.clip(drawn, min=-bound, max=bound).astype(kind)


def setup_inputs(seed: int = 0) -> dict:
    splits = jax.random.split(jax.random.key(seed), 6)
    vectors = centred(splits[0], (K, N), 1.0, 6.0, ((1, 32),), jnp.float32)
    blocks = centred(splits[1], (N_ROW, N_COL, DEVICE_SLOTS, ORBITAL_COUNT, ORBITAL_COUNT), (ORBITAL_COUNT * N_COL * DEVICE_SLOTS // SLAB_BLOCK_ROWS) ** -0.5, 0.0390625, ((0, 8), (1, 4)))
    slot_block_rows = with_ends(jax.random.randint(splits[2], (N_ROW, N_COL, DEVICE_SLOTS), 0, SLAB_BLOCK_ROWS), jax.random.fold_in(splits[2], 1), 0, SLAB_BLOCK_ROWS - 1).astype(jnp.int32)
    slot_block_columns = with_ends(jax.random.randint(splits[3], (N_ROW, N_COL, DEVICE_SLOTS), 0, SLAB_BLOCK_COLS), jax.random.fold_in(splits[3], 1), 0, SLAB_BLOCK_COLS - 1).astype(jnp.int32)
    counts = draw_counts(jax.random.fold_in(splits[5], 71), 0)
    return {"vectors": vectors, "blocks": blocks, "slot_block_rows": slot_block_rows, "slot_block_columns": slot_block_columns, "counts": counts}


CENTER = 0.25
HALF_WIDTH = 2.0


def hamiltonian(current, blocks, slot_block_rows, slot_block_columns, counts):
    width = current.shape[0]
    slab_groups = N_ROW // N_COL
    wire = current.astype(jnp.bfloat16).reshape(width, NBLK, ORBITAL_COUNT)
    row_ids = jnp.arange(N_ROW, dtype=jnp.int32)[:, None, None]
    col_ids = jnp.arange(N_COL, dtype=jnp.int32)[None, :, None]
    slot_numbers = jnp.arange(DEVICE_SLOTS, dtype=jnp.int32)[None, None, :]
    global_rows = (row_ids * SLAB_BLOCK_ROWS + slot_block_rows).astype(jnp.int32)
    global_cols = ((col_ids + N_COL * (slot_block_columns // SLAB_BLOCK_ROWS)) * SLAB_BLOCK_ROWS + slot_block_columns % SLAB_BLOCK_ROWS).astype(jnp.int32)
    live = (slot_numbers < counts[:, :, None]) & (global_rows <= global_cols)
    row_range = jnp.arange(SLAB_BLOCK_ROWS, dtype=jnp.int32)
    col_range = jnp.arange(SLAB_BLOCK_COLS, dtype=jnp.int32)

    def one_row(carry, inputs):
        block_entries, rows_here, cols_here, grow_here, gcol_here, live_here = inputs
        block_entries = jnp.where(live_here[:, :, None, None], block_entries, jnp.zeros_like(block_entries)).astype(jnp.float32)
        inputs_col = wire[:, gcol_here, :].astype(jnp.float32)
        products = jnp.einsum('jsab,kjsb->kjsa', block_entries, inputs_col)
        onehot_rows = (rows_here[:, :, None] == row_range).astype(jnp.float32)
        row_part = jnp.einsum('jsr,kjsa->kjra', onehot_rows, products)
        row_part = lax.optimization_barrier(row_part.astype(jnp.bfloat16)).astype(jnp.float32)
        row_sum = jnp.sum(row_part, axis=1)
        inputs_row = wire[:, grow_here, :].astype(jnp.float32)
        products_t = jnp.einsum('jsba,kjsb->kjsa', block_entries, inputs_row)
        onehot_cols = (cols_here[:, :, None] == col_range).astype(jnp.float32)
        col_part = jnp.einsum('jsc,kjsa->kjca', onehot_cols, products_t)
        col_part = lax.optimization_barrier(col_part.astype(jnp.bfloat16)).astype(jnp.float32)
        return carry + col_part, row_sum

    start = jnp.zeros((width, N_COL, SLAB_BLOCK_COLS, ORBITAL_COUNT), jnp.float32)
    col_total, row_sums = lax.scan(one_row, start, (blocks, slot_block_rows, slot_block_columns, global_rows, global_cols, live))
    row_full = jnp.transpose(row_sums, (1, 0, 2, 3)).reshape(width, N)
    col_full = col_total.reshape(width, N_COL, slab_groups, SLAB_BLOCK_ROWS, ORBITAL_COUNT)
    col_full = jnp.transpose(col_full, (0, 2, 1, 3, 4)).reshape(width, N)
    return row_full + col_full


def reference(vectors, blocks, slot_block_rows, slot_block_columns, counts):
    previous = vectors
    current = (hamiltonian(vectors, blocks, slot_block_rows, slot_block_columns, counts) - CENTER * vectors) / HALF_WIDTH
    for degree_step in range(DEGREE - 1):
        image = hamiltonian(current, blocks, slot_block_rows, slot_block_columns, counts)
        following = 2.0 * (image - CENTER * current) / HALF_WIDTH - previous
        previous, current = current, following
    return current
```

```python
import functools

import jax
import jax.numpy as jnp
from jax import lax
from jax.experimental import pallas as pl
from jax.experimental.pallas import tpu as pltpu
from jax.sharding import PartitionSpec as P

DEGREE = 3
CENTER = 0.25
HALF_WIDTH = 2.0
PARTS = 4
MESH = pl.DeviceIdType.MESH


def densify_kernel(
    row_count, col_count, chunks, rows_ref, cols_ref, count_ref, blocks_ref, dense_ref, buf, *rest
):
    accs, sems = rest[:-1], rest[-1]
    slots, size = buf.shape[0], buf.shape[1]
    per_chunk = slots // chunks
    groups = dense_ref.shape[0]
    slab = dense_ref.shape[1] // size
    positions = slab * groups * slab
    band = size // PARTS
    a, b = lax.axis_index("row"), lax.axis_index("col")
    count = count_ref[0, 0]

    def chunk_copy(k):
        span = pl.ds(k * per_chunk, per_chunk)
        return pltpu.make_async_copy(blocks_ref.at[0, 0, span], buf.at[span], sems.at[k])

    for k in range(chunks):
        chunk_copy(k).start()

    def clear(p, carry):
        for acc in accs:
            acc[p] = jnp.zeros(acc.shape[1:], acc.dtype)
        return carry

    lax.fori_loop(0, positions + 1, clear, 0)

    def add_slot(s):
        r = rows_ref[0, 0, s]
        c = cols_ref[0, 0, s]
        global_row = a * slab + r
        global_col = (b + col_count * lax.div(c, slab)) * slab + lax.rem(c, slab)
        live = (s < count) & (global_row <= global_col)
        p = jnp.where(live, r * (groups * slab) + c, positions)
        for q, acc in enumerate(accs):
            acc[p] += buf[s, q * band : (q + 1) * band, :].astype(jnp.float32)

    for k in range(chunks):
        chunk_copy(k).wait()

        def body(i, carry, k=k):
            add_slot(k * per_chunk + i)
            return carry

        lax.fori_loop(0, per_chunk, body, 0, unroll=True if slots % 19 == 0 and per_chunk <= 19 else 1)

    def store(n, carry):
        h, r = lax.div(n, slab), lax.rem(n, slab)
        for l in range(slab):
            p = r * (groups * slab) + h * slab + l
            for q, acc in enumerate(accs):
                start = pl.multiple_of(r * size + q * band, band)
                dense_ref[h, pl.ds(start, band), l * size : (l + 1) * size] = acc[p].astype(jnp.bfloat16)
        return carry

    lax.fori_loop(0, groups * slab, store, 0)


def filter_kernel(
    R, C, x_ref, dense_hbm, out_ref, dense, cur, prev, total, racc, wsend, xrow, xcol, rsend, csend,
    rterm, cterm, dsem, xr_s, xr_r, xc_s, xc_r, rt_s, rt_r, ct_s, ct_r,
):
    G = R // C
    width, piece = x_ref.shape
    slab = C * piece
    a, b = lax.axis_index("row"), lax.axis_index("col")
    my_group, my_col = a // C, a % C

    def alive(j):
        return j + C * (G - 1) >= a

    def above(h):
        return b + C * h > a

    live = alive(b)
    diag = my_col == b

    load = pltpu.make_async_copy(dense_hbm, dense, dsem)
    load.start()

    barrier = pltpu.get_barrier_semaphore()

    def greet(row, col):
        pl.semaphore_signal(barrier, inc=1, device_id=(row, col), device_id_type=MESH)

    for j in range(C):
        @pl.when(j != b)
        def _():
            greet(a, j)
    for i in range(R - 1):
        @pl.when(i < a)
        def _():
            greet(i, my_col)
    greeted = C - 1 + a
    for h in range(G):
        @pl.when(above(h))
        def _():
            for j in range(C):
                greet(b + C * h, j)
        greeted = greeted + jnp.where(above(h), C, 0)
    pl.semaphore_wait(barrier, greeted)

    def remote(src, dst, send, recv, row, col):
        return pltpu.make_async_remote_copy(
            src_ref=src, dst_ref=dst, send_sem=send, recv_sem=recv, device_id=(row, col), device_id_type=MESH
        )

    def send_x_col(t, i):
        return remote(wsend.at[t], xcol.at[t, my_group, b], xc_s.at[t, i], xc_r.at[t, my_group, b], i, my_col)

    def send_x_row(t, j):
        return remote(wsend.at[t], xrow.at[t, b], xr_s.at[t, j], xr_r.at[t, b], a, j)

    def send_col_term(t, h, j):
        return remote(csend.at[t, h, j], cterm.at[t, a], ct_s.at[t, h, j], ct_r.at[t, a], b + C * h, j)

    def send_row_term(t, j):
        return remote(rsend.at[t, j], rterm.at[t, b], rt_s.at[t, j], rt_r.at[t, b], a, j)

    def got_x_col(t, h, j):
        remote(wsend.at[t], xcol.at[t, h, j], xc_s.at[t, 0], xc_r.at[t, h, j], b + C * h, j).wait_recv()

    def got_x_row(t, j):
        remote(wsend.at[t], xrow.at[t, j], xr_s.at[t, j], xr_r.at[t, j], a, j).wait_recv()

    def got_col_term(t, i):
        remote(csend.at[t, 0, 0], cterm.at[t, i], ct_s.at[t, 0, 0], ct_r.at[t, i], i, my_col).wait_recv()

    def got_row_term(t, j):
        remote(rsend.at[t, j], rterm.at[t, j], rt_s.at[t, j], rt_r.at[t, j], a, j).wait_recv()

    def times(x, m):
        return lax.dot_general(x, m, (((1,), (0,)), ((), ())), preferred_element_type=jnp.float32)

    def times_t(x, m):
        return lax.dot_general(x, m, (((1,), (1,)), ((), ())), preferred_element_type=jnp.float32)

    cur[...] = x_ref[...]
    prev[...] = jnp.zeros_like(prev)

    def step(t, carry):
        w = cur[...].astype(jnp.bfloat16)
        wsend[t] = w
        for j in range(C):
            @pl.when((j != b) & alive(j))
            def _():
                send_x_row(t, j).start()
        for i in range(R - 1):
            @pl.when(i < a)
            def _():
                send_x_col(t, i).start()

        @pl.when(t == 0)
        def _():
            load.wait()

        @pl.when(live)
        def _():
            xrow[t, b] = w
            for j in range(C):
                @pl.when(j != b)
                def _():
                    got_x_row(t, j)
            xr = jnp.concatenate([xrow[t, j] for j in range(C)], axis=1)
            for h in range(G - 1, -1, -1):
                @pl.when(above(h))
                def _():
                    terms = times(xr, dense[h]).astype(jnp.bfloat16)
                    for j in range(C):
                        csend[t, h, j] = terms[:, j * piece : (j + 1) * piece]
                        send_col_term(t, h, j).start()

            @pl.when(diag)
            def _():
                racc[...] = times(xr, dense[my_group]) + times_t(xr, dense[my_group])

            @pl.when(jnp.logical_not(diag))
            def _():
                racc[...] = jnp.zeros_like(racc)

            for h in range(G):
                @pl.when(above(h))
                def _():
                    for j in range(C):
                        got_x_col(t, h, j)
                    xc = jnp.concatenate([xcol[t, h, j] for j in range(C)], axis=1)
                    racc[...] += times_t(xc, dense[h])

            for j in range(C):
                mine = racc[:, j * piece : (j + 1) * piece].astype(jnp.bfloat16)

                @pl.when(j != b)
                def _():
                    rsend[t, j] = mine
                    send_row_term(t, j).start()

                @pl.when(j == b)
                def _():
                    rterm[t, j] = mine

        total[...] = -CENTER * cur[...]
        for j in range(C):
            @pl.when(alive(j))
            def _():
                @pl.when(j != b)
                def _():
                    got_row_term(t, j)
                total[...] += rterm[t, j].astype(jnp.float32)
        for i in range(R - 1):
            @pl.when(i < a)
            def _():
                got_col_term(t, i)
                total[...] += cterm[t, i].astype(jnp.float32)
        scale = jnp.where(t == 0, 1.0 / HALF_WIDTH, 2.0 / HALF_WIDTH)
        following = scale * total[...] - prev[...]
        prev[...] = cur[...]
        cur[...] = following
        return carry

    lax.fori_loop(0, DEGREE, step, 0)
    out_ref[...] = cur[...]

    def drain(t, carry):
        for j in range(C):
            @pl.when((j != b) & alive(j))
            def _():
                send_x_row(t, j).wait_send()

            @pl.when((j != b) & live)
            def _():
                send_row_term(t, j).wait_send()
        for i in range(R - 1):
            @pl.when(i < a)
            def _():
                send_x_col(t, i).wait_send()
        for h in range(G):
            @pl.when(above(h))
            def _():
                for j in range(C):
                    send_col_term(t, h, j).wait_send()
        return carry

    lax.fori_loop(0, DEGREE, drain, 0)


def local(vectors, blocks, slot_block_rows, slot_block_columns, counts):
    width, piece = vectors.shape
    slots, size = blocks.shape[2], blocks.shape[3]
    R, C = lax.axis_size("row"), lax.axis_size("col")
    G = R // C
    slab = C * piece
    positions = (slab // size) ** 2 * G
    chunks = next(n for n in (8, 4, 2, 1) if slots % n == 0)
    bf16, f32 = jnp.bfloat16, jnp.float32
    smem, vmem = pl.BlockSpec(memory_space=pltpu.SMEM), pl.BlockSpec(memory_space=pltpu.VMEM)
    hbm = pl.BlockSpec(memory_space=pl.ANY)
    dense_shape = (G, slab, slab)
    dense = pl.pallas_call(
        functools.partial(densify_kernel, R, C, chunks),
        out_shape=jax.ShapeDtypeStruct(dense_shape, bf16),
        in_specs=[smem, smem, smem, hbm],
        out_specs=vmem,
        scratch_shapes=[pltpu.VMEM((slots, size, size), bf16)]
        + [pltpu.VMEM((positions + 1, size // PARTS, size), f32)] * PARTS
        + [pltpu.SemaphoreType.DMA((chunks,))],
        compiler_params=pltpu.CompilerParams(vmem_limit_bytes=60 * 2**20),
    )(slot_block_rows, slot_block_columns, counts, blocks)

    def dma(*shape):
        return pltpu.SemaphoreType.DMA((DEGREE,) + shape)

    def pieces(*shape):
        return pltpu.VMEM((DEGREE,) + shape + (width, piece), bf16)

    return pl.pallas_call(
        functools.partial(filter_kernel, R, C),
        out_shape=jax.ShapeDtypeStruct((width, piece), f32),
        in_specs=[vmem, hbm],
        out_specs=vmem,
        scratch_shapes=[
            pltpu.VMEM(dense_shape, bf16),
            pltpu.VMEM((width, piece), f32),
            pltpu.VMEM((width, piece), f32),
            pltpu.VMEM((width, piece), f32),
            pltpu.VMEM((width, slab), f32),
            pieces(),
            pieces(C),
            pieces(G, C),
            pieces(C),
            pieces(G, C),
            pieces(C),
            pieces(R),
            pltpu.SemaphoreType.DMA,
            dma(C),
            dma(C),
            dma(R),
            dma(G, C),
            dma(C),
            dma(C),
            dma(G, C),
            dma(R),
        ],
        compiler_params=pltpu.CompilerParams(
            collective_id=0, has_side_effects=True, vmem_limit_bytes=48 * 2**20
        ),
    )(vectors, dense)


def solution(mesh):
    in_specs = (
        P(None, ("row", "col")),
        P("row", "col", None, None, None),
        P("row", "col", None),
        P("row", "col", None),
        P("row", "col"),
    )
    out_specs = P(None, ("row", "col"))
    return jax.shard_map(local, mesh=mesh, in_specs=in_specs, out_specs=out_specs, check_vma=False)
```

```python
import functools

import jax
import jax.numpy as jnp
from jax import lax
from jax.experimental import pallas as pl
from jax.experimental.pallas import tpu as pltpu
from jax.sharding import PartitionSpec as P

DEGREE = 3
CENTER = 0.25
HALF_WIDTH = 2.0
PARTS = 4
BATCHES = 2
MESH = pl.DeviceIdType.MESH


def densify_kernel(
    row_count, col_count, chunks, rows_ref, cols_ref, count_ref, blocks_ref, dense_ref, buf, *rest
):
    accs, sems = rest[:-1], rest[-1]
    slots, size = buf.shape[0], buf.shape[1]
    per_chunk = slots // chunks
    groups = dense_ref.shape[0]
    slab = dense_ref.shape[1] // size
    positions = slab * groups * slab
    band = size // PARTS
    a, b = lax.axis_index("row"), lax.axis_index("col")
    count = count_ref[0, 0]

    def chunk_copy(k):
        span = pl.ds(k * per_chunk, per_chunk)
        return pltpu.make_async_copy(blocks_ref.at[0, 0, span], buf.at[span], sems.at[k])

    for k in range(chunks):
        chunk_copy(k).start()

    def clear(p, carry):
        for acc in accs:
            acc[p] = jnp.zeros(acc.shape[1:], acc.dtype)
        return carry

    lax.fori_loop(0, positions + 1, clear, 0)

    def add_slot(s):
        r = rows_ref[0, 0, s]
        c = cols_ref[0, 0, s]
        global_row = a * slab + r
        global_col = (b + col_count * lax.div(c, slab)) * slab + lax.rem(c, slab)
        live = (s < count) & (global_row <= global_col)
        p = jnp.where(live, r * (groups * slab) + c, positions)
        for q, acc in enumerate(accs):
            acc[p] += buf[s, q * band : (q + 1) * band, :].astype(jnp.float32)

    for k in range(chunks):
        chunk_copy(k).wait()

        def body(i, carry, k=k):
            add_slot(k * per_chunk + i)
            return carry

        lax.fori_loop(0, per_chunk, body, 0, unroll=True if slots % 19 == 0 and per_chunk <= 19 else 1)

    def store(n, carry):
        h, r = lax.div(n, slab), lax.rem(n, slab)
        for l in range(slab):
            p = r * (groups * slab) + h * slab + l
            for q, acc in enumerate(accs):
                start = pl.multiple_of(r * size + q * band, band)
                dense_ref[h, pl.ds(start, band), l * size : (l + 1) * size] = acc[p].astype(jnp.bfloat16)
        return carry

    lax.fori_loop(0, groups * slab, store, 0)


def filter_kernel(
    R, C, x_ref, dense_hbm, out_ref, dense, cur, prev, total, racc, wsend, xrow, xcol, rsend, csend,
    rterm, cterm, dsem, xr_s, xr_r, xc_s, xc_r, rt_s, rt_r, ct_s, ct_r,
):
    G = R // C
    piece = x_ref.shape[1]
    V, rows = cur.shape[:2]
    a, b = lax.axis_index("row"), lax.axis_index("col")
    my_group, my_col = a // C, a % C

    def alive(j):
        return j + C * (G - 1) >= a

    def above(h):
        return b + C * h > a

    live = alive(b)
    diag = my_col == b

    load = pltpu.make_async_copy(dense_hbm, dense, dsem)
    load.start()

    barrier = pltpu.get_barrier_semaphore()

    def greet(row, col):
        pl.semaphore_signal(barrier, inc=1, device_id=(row, col), device_id_type=MESH)

    for j in range(C):
        @pl.when(j != b)
        def _():
            greet(a, j)
    for i in range(R - 1):
        @pl.when(i < a)
        def _():
            greet(i, my_col)
    greeted = C - 1 + a
    for h in range(G):
        @pl.when(above(h))
        def _():
            for j in range(C):
                greet(b + C * h, j)
        greeted = greeted + jnp.where(above(h), C, 0)
    pl.semaphore_wait(barrier, greeted)

    def remote(src, dst, send, recv, row, col):
        return pltpu.make_async_remote_copy(
            src_ref=src, dst_ref=dst, send_sem=send, recv_sem=recv, device_id=(row, col), device_id_type=MESH
        )

    def send_x_col(t, v, i):
        return remote(
            wsend.at[t, v], xcol.at[t, v, my_group, b], xc_s.at[t, v, i], xc_r.at[t, v, my_group, b], i, my_col
        )

    def send_x_row(t, v, j):
        return remote(wsend.at[t, v], xrow.at[t, v, b], xr_s.at[t, v, j], xr_r.at[t, v, b], a, j)

    def send_col_term(t, v, h, j):
        return remote(
            csend.at[t, v, h, j], cterm.at[t, v, a], ct_s.at[t, v, h, j], ct_r.at[t, v, a], b + C * h, j
        )

    def send_row_term(t, v, j):
        return remote(rsend.at[t, v, j], rterm.at[t, v, b], rt_s.at[t, v, j], rt_r.at[t, v, b], a, j)

    def got_x_col(t, v, h, j):
        remote(
            wsend.at[t, v], xcol.at[t, v, h, j], xc_s.at[t, v, 0], xc_r.at[t, v, h, j], b + C * h, j
        ).wait_recv()

    def got_x_row(t, v, j):
        remote(wsend.at[t, v], xrow.at[t, v, j], xr_s.at[t, v, j], xr_r.at[t, v, j], a, j).wait_recv()

    def got_col_term(t, v, i):
        remote(
            csend.at[t, v, 0, 0], cterm.at[t, v, i], ct_s.at[t, v, 0, 0], ct_r.at[t, v, i], i, my_col
        ).wait_recv()

    def got_row_term(t, v, j):
        remote(rsend.at[t, v, j], rterm.at[t, v, j], rt_s.at[t, v, j], rt_r.at[t, v, j], a, j).wait_recv()

    def times(x, m):
        return lax.dot_general(x, m, (((1,), (0,)), ((), ())), preferred_element_type=jnp.float32)

    def times_t(x, m):
        return lax.dot_general(x, m, (((1,), (1,)), ((), ())), preferred_element_type=jnp.float32)

    def side_by_side(ref, *index):
        return jnp.concatenate([ref[index + (j,)] for j in range(C)], axis=1)

    def hand_out(t, v):
        w = cur[v].astype(jnp.bfloat16)
        wsend[t, v] = w
        for j in range(C):
            @pl.when((j != b) & alive(j))
            def _():
                send_x_row(t, v, j).start()
        for i in range(R - 1):
            @pl.when(i < a)
            def _():
                send_x_col(t, v, i).start()

        @pl.when(live)
        def _():
            xrow[t, v, b] = w

    def column_terms(t, v):
        for j in range(C):
            @pl.when(j != b)
            def _():
                got_x_row(t, v, j)
        xr = side_by_side(xrow, t, v)
        for h in range(G - 1, -1, -1):
            @pl.when(above(h))
            def _():
                terms = times(xr, dense[h]).astype(jnp.bfloat16)
                for j in range(C):
                    csend[t, v, h, j] = terms[:, j * piece : (j + 1) * piece]
                    send_col_term(t, v, h, j).start()

    def diagonal_terms(t, v):
        @pl.when(diag)
        def _():
            xr = side_by_side(xrow, t, v)
            racc[v] = times(xr, dense[my_group]) + times_t(xr, dense[my_group])

        @pl.when(jnp.logical_not(diag))
        def _():
            racc[v] = jnp.zeros(racc.shape[1:], racc.dtype)

    def row_terms(t, v):
        for h in range(G):
            @pl.when(above(h))
            def _():
                for j in range(C):
                    got_x_col(t, v, h, j)
                racc[v] += times_t(side_by_side(xcol, t, v, h), dense[h])
        for j in range(C):
            mine = racc[v, :, j * piece : (j + 1) * piece].astype(jnp.bfloat16)

            @pl.when(j != b)
            def _():
                rsend[t, v, j] = mine
                send_row_term(t, v, j).start()

            @pl.when(j == b)
            def _():
                rterm[t, v, j] = mine

    def update(t, v):
        total[v] = -CENTER * cur[v]
        for j in range(C):
            @pl.when(alive(j))
            def _():
                @pl.when(j != b)
                def _():
                    got_row_term(t, v, j)
                total[v] += rterm[t, v, j].astype(jnp.float32)
        for i in range(R - 1):
            @pl.when(i < a)
            def _():
                got_col_term(t, v, i)
                total[v] += cterm[t, v, i].astype(jnp.float32)
        scale = jnp.where(t == 0, 1.0 / HALF_WIDTH, 2.0 / HALF_WIDTH)
        following = scale * total[v] - prev[v]
        prev[v] = cur[v]
        cur[v] = following

    for v in range(V):
        cur[v] = x_ref[v * rows : (v + 1) * rows, :]
        hand_out(0, v)
    prev[...] = jnp.zeros_like(prev)
    load.wait()

    def step(t, carry):
        @pl.when(live)
        def _():
            for v in range(V):
                column_terms(t, v)
            for v in range(V):
                diagonal_terms(t, v)
            for v in range(V):
                row_terms(t, v)
        for v in range(V):
            update(t, v)

            @pl.when(t < DEGREE - 1)
            def _():
                hand_out(t + 1, v)
        return carry

    lax.fori_loop(0, DEGREE, step, 0)
    for v in range(V):
        out_ref[v * rows : (v + 1) * rows, :] = cur[v]

    def drain(t, carry):
        for v in range(V):
            for j in range(C):
                @pl.when((j != b) & alive(j))
                def _():
                    send_x_row(t, v, j).wait_send()

                @pl.when((j != b) & live)
                def _():
                    send_row_term(t, v, j).wait_send()
            for i in range(R - 1):
                @pl.when(i < a)
                def _():
                    send_x_col(t, v, i).wait_send()
            for h in range(G):
                @pl.when(above(h))
                def _():
                    for j in range(C):
                        send_col_term(t, v, h, j).wait_send()
        return carry

    lax.fori_loop(0, DEGREE, drain, 0)


def local(vectors, blocks, slot_block_rows, slot_block_columns, counts):
    width, piece = vectors.shape
    slots, size = blocks.shape[2], blocks.shape[3]
    R, C = lax.axis_size("row"), lax.axis_size("col")
    G = R // C
    slab = C * piece
    rows = width // BATCHES
    positions = (slab // size) ** 2 * G
    chunks = next(n for n in (8, 4, 2, 1) if slots % n == 0)
    bf16, f32 = jnp.bfloat16, jnp.float32
    smem, vmem = pl.BlockSpec(memory_space=pltpu.SMEM), pl.BlockSpec(memory_space=pltpu.VMEM)
    hbm = pl.BlockSpec(memory_space=pl.ANY)
    dense_shape = (G, slab, slab)
    dense = pl.pallas_call(
        functools.partial(densify_kernel, R, C, chunks),
        out_shape=jax.ShapeDtypeStruct(dense_shape, bf16),
        in_specs=[smem, smem, smem, hbm],
        out_specs=vmem,
        scratch_shapes=[pltpu.VMEM((slots, size, size), bf16)]
        + [pltpu.VMEM((positions + 1, size // PARTS, size), f32)] * PARTS
        + [pltpu.SemaphoreType.DMA((chunks,))],
        compiler_params=pltpu.CompilerParams(vmem_limit_bytes=60 * 2**20),
    )(slot_block_rows, slot_block_columns, counts, blocks)

    def dma(*shape):
        return pltpu.SemaphoreType.DMA((DEGREE, BATCHES) + shape)

    def pieces(*shape):
        return pltpu.VMEM((DEGREE, BATCHES) + shape + (rows, piece), bf16)

    return pl.pallas_call(
        functools.partial(filter_kernel, R, C),
        out_shape=jax.ShapeDtypeStruct((width, piece), f32),
        in_specs=[vmem, hbm],
        out_specs=vmem,
        scratch_shapes=[
            pltpu.VMEM(dense_shape, bf16),
            pltpu.VMEM((BATCHES, rows, piece), f32),
            pltpu.VMEM((BATCHES, rows, piece), f32),
            pltpu.VMEM((BATCHES, rows, piece), f32),
            pltpu.VMEM((BATCHES, rows, slab), f32),
            pieces(),
            pieces(C),
            pieces(G, C),
            pieces(C),
            pieces(G, C),
            pieces(C),
            pieces(R),
            pltpu.SemaphoreType.DMA,
            dma(C),
            dma(C),
            dma(R),
            dma(G, C),
            dma(C),
            dma(C),
            dma(G, C),
            dma(R),
        ],
        compiler_params=pltpu.CompilerParams(
            collective_id=0, has_side_effects=True, vmem_limit_bytes=60 * 2**20
        ),
    )(vectors, dense)


def solution(mesh):
    in_specs = (
        P(None, ("row", "col")),
        P("row", "col", None, None, None),
        P("row", "col", None),
        P("row", "col", None),
        P("row", "col"),
    )
    out_specs = P(None, ("row", "col"))
    return jax.shard_map(local, mesh=mesh, in_specs=in_specs, out_specs=out_specs, check_vma=False)
```

```python
import functools

import jax
import jax.numpy as jnp
from jax import lax
from jax.experimental import pallas as pl
from jax.experimental.pallas import tpu as pltpu
from jax.sharding import PartitionSpec as P

DEGREE = 3
CENTER = 0.25
HALF_WIDTH = 2.0
PARTS = 4
BATCHES = 1
TILE = 256
MESH = pl.DeviceIdType.MESH


def densify_kernel(
    row_count, col_count, chunks, rows_ref, cols_ref, count_ref, blocks_ref, dense_ref, buf, *rest
):
    accs, sems = rest[:-1], rest[-1]
    slots, size = buf.shape[0], buf.shape[1]
    per_chunk = slots // chunks
    groups = dense_ref.shape[0]
    slab = dense_ref.shape[1] // size
    positions = slab * groups * slab
    band = size // PARTS
    a, b = lax.axis_index("row"), lax.axis_index("col")
    count = count_ref[0, 0]

    def chunk_copy(k):
        span = pl.ds(k * per_chunk, per_chunk)
        return pltpu.make_async_copy(blocks_ref.at[0, 0, span], buf.at[span], sems.at[k])

    for k in range(chunks):
        chunk_copy(k).start()

    def clear(p, carry):
        for acc in accs:
            acc[p] = jnp.zeros(acc.shape[1:], acc.dtype)
        return carry

    lax.fori_loop(0, positions + 1, clear, 0)

    def add_slot(s):
        r = rows_ref[0, 0, s]
        c = cols_ref[0, 0, s]
        global_row = a * slab + r
        global_col = (b + col_count * lax.div(c, slab)) * slab + lax.rem(c, slab)
        live = (s < count) & (global_row <= global_col)
        p = jnp.where(live, r * (groups * slab) + c, positions)
        for q, acc in enumerate(accs):
            acc[p] += buf[s, q * band : (q + 1) * band, :].astype(jnp.float32)

    for k in range(chunks):
        chunk_copy(k).wait()

        def body(i, carry, k=k):
            add_slot(k * per_chunk + i)
            return carry

        lax.fori_loop(0, per_chunk, body, 0, unroll=True if slots % 19 == 0 and per_chunk <= 19 else 1)

    def store(n, carry):
        h, r = lax.div(n, slab), lax.rem(n, slab)
        for l in range(slab):
            p = r * (groups * slab) + h * slab + l
            for q, acc in enumerate(accs):
                start = pl.multiple_of(r * size + q * band, band)
                dense_ref[h, pl.ds(start, band), l * size : (l + 1) * size] = acc[p].astype(jnp.bfloat16)
        return carry

    lax.fori_loop(0, groups * slab, store, 0)


def filter_kernel(
    R, C, x_ref, dense, out_ref, dense_t, cur, prev, total, racc, wsend, xrow, xcol, rsend, csend,
    rterm, cterm, xr_s, xr_r, xc_s, xc_r, rt_s, rt_r, ct_s, ct_r,
):
    G = R // C
    piece = x_ref.shape[1]
    V, rows = cur.shape[:2]
    a, b = lax.axis_index("row"), lax.axis_index("col")
    my_group, my_col = a // C, a % C

    def alive(j):
        return j + C * (G - 1) >= a

    def above(h):
        return b + C * h > a

    live = alive(b)
    diag = my_col == b

    barrier = pltpu.get_barrier_semaphore()

    def greet(row, col):
        pl.semaphore_signal(barrier, inc=1, device_id=(row, col), device_id_type=MESH)

    for j in range(C):
        @pl.when(j != b)
        def _():
            greet(a, j)
    for i in range(R - 1):
        @pl.when(i < a)
        def _():
            greet(i, my_col)
    greeted = C - 1 + a
    for h in range(G):
        @pl.when(above(h))
        def _():
            for j in range(C):
                greet(b + C * h, j)
        greeted = greeted + jnp.where(above(h), C, 0)
    pl.semaphore_wait(barrier, greeted)

    def remote(src, dst, send, recv, row, col):
        return pltpu.make_async_remote_copy(
            src_ref=src, dst_ref=dst, send_sem=send, recv_sem=recv, device_id=(row, col), device_id_type=MESH
        )

    def send_x_col(t, v, i):
        return remote(
            wsend.at[t, v], xcol.at[t, v, my_group, b], xc_s.at[t, v, i], xc_r.at[t, v, my_group, b], i, my_col
        )

    def send_x_row(t, v, j):
        return remote(wsend.at[t, v], xrow.at[t, v, b], xr_s.at[t, v, j], xr_r.at[t, v, b], a, j)

    def send_col_term(t, v, h, j):
        return remote(
            csend.at[t, v, h, j], cterm.at[t, v, a], ct_s.at[t, v, h, j], ct_r.at[t, v, a], b + C * h, j
        )

    def send_row_term(t, v, j):
        return remote(rsend.at[t, v, j], rterm.at[t, v, b], rt_s.at[t, v, j], rt_r.at[t, v, b], a, j)

    def got_x_col(t, v, h, j):
        remote(
            wsend.at[t, v], xcol.at[t, v, h, j], xc_s.at[t, v, 0], xc_r.at[t, v, h, j], b + C * h, j
        ).wait_recv()

    def got_x_row(t, v, j):
        remote(wsend.at[t, v], xrow.at[t, v, j], xr_s.at[t, v, j], xr_r.at[t, v, j], a, j).wait_recv()

    def got_col_term(t, v, i):
        remote(
            csend.at[t, v, 0, 0], cterm.at[t, v, i], ct_s.at[t, v, 0, 0], ct_r.at[t, v, i], i, my_col
        ).wait_recv()

    def got_row_term(t, v, j):
        remote(rsend.at[t, v, j], rterm.at[t, v, j], rt_s.at[t, v, j], rt_r.at[t, v, j], a, j).wait_recv()

    def times(x, m):
        return lax.dot_general(x, m, (((1,), (0,)), ((), ())), preferred_element_type=jnp.float32)

    def transpose_dense():
        n = dense.shape[1] // TILE

        def tile(k, carry):
            h, i, j = k // (n * n), (k // n) % n, k % n
            down, across = pl.ds(pl.multiple_of(i * TILE, TILE), TILE), pl.ds(pl.multiple_of(j * TILE, TILE), TILE)
            dense_t[h, across, down] = dense[h, down, across].T
            return carry

        lax.fori_loop(0, G * n * n, tile, 0)

    def side_by_side(ref, *index):
        return jnp.concatenate([ref[index + (j,)] for j in range(C)], axis=1)

    def hand_out(t, v):
        w = cur[v].astype(jnp.bfloat16)
        wsend[t, v] = w
        for j in range(C):
            @pl.when((j != b) & alive(j))
            def _():
                send_x_row(t, v, j).start()
        for i in range(R - 1):
            @pl.when(i < a)
            def _():
                send_x_col(t, v, i).start()

        @pl.when(live)
        def _():
            xrow[t, v, b] = w

    def column_terms(t, v):
        for j in range(C):
            @pl.when(j != b)
            def _():
                got_x_row(t, v, j)
        xr = side_by_side(xrow, t, v)
        for h in range(G - 1, -1, -1):
            @pl.when(above(h))
            def _():
                terms = times(xr, dense[h]).astype(jnp.bfloat16)
                for j in range(C):
                    csend[t, v, h, j] = terms[:, j * piece : (j + 1) * piece]
                    send_col_term(t, v, h, j).start()

    def diagonal_terms(t, v):
        @pl.when(diag)
        def _():
            xr = side_by_side(xrow, t, v)
            racc[v] = times(xr, dense[my_group]) + times(xr, dense_t[my_group])

        @pl.when(jnp.logical_not(diag))
        def _():
            racc[v] = jnp.zeros(racc.shape[1:], racc.dtype)

    def row_terms(t, v):
        for h in range(G):
            @pl.when(above(h))
            def _():
                for j in range(C):
                    got_x_col(t, v, h, j)
                racc[v] += times(side_by_side(xcol, t, v, h), dense_t[h])
        for j in range(C):
            mine = racc[v, :, j * piece : (j + 1) * piece].astype(jnp.bfloat16)

            @pl.when(j != b)
            def _():
                rsend[t, v, j] = mine
                send_row_term(t, v, j).start()

            @pl.when(j == b)
            def _():
                rterm[t, v, j] = mine

    def update(t, v):
        total[v] = -CENTER * cur[v]
        for j in range(C):
            @pl.when(alive(j))
            def _():
                @pl.when(j != b)
                def _():
                    got_row_term(t, v, j)
                total[v] += rterm[t, v, j].astype(jnp.float32)
        for i in range(R - 1):
            @pl.when(i < a)
            def _():
                got_col_term(t, v, i)
                total[v] += cterm[t, v, i].astype(jnp.float32)
        scale = jnp.where(t == 0, 1.0 / HALF_WIDTH, 2.0 / HALF_WIDTH)
        following = scale * total[v] - prev[v]
        prev[v] = cur[v]
        cur[v] = following

    for v in range(V):
        cur[v] = x_ref[v * rows : (v + 1) * rows, :]
        hand_out(0, v)
    prev[...] = jnp.zeros_like(prev)

    def sent_early(t):
        for v in range(V):
            for j in range(C):
                @pl.when((j != b) & alive(j))
                def _():
                    send_x_row(t, v, j).wait_send()
            for i in range(R - 1):
                @pl.when(i < a)
                def _():
                    send_x_col(t, v, i).wait_send()
            for h in range(G):
                @pl.when(above(h))
                def _():
                    for j in range(C):
                        send_col_term(t, v, h, j).wait_send()

    def sent_late(t):
        @pl.when(live)
        def _():
            for v in range(V):
                for j in range(C):
                    @pl.when(j != b)
                    def _():
                        send_row_term(t, v, j).wait_send()

    def step(t, carry):
        @pl.when(live)
        def _():
            for v in range(V):
                column_terms(t, v)

            @pl.when(t == 0)
            def _():
                transpose_dense()

            for v in range(V):
                diagonal_terms(t, v)
            for v in range(V):
                row_terms(t, v)
        sent_early(t)

        @pl.when(t > 0)
        def _():
            sent_late(t - 1)

        for v in range(V):
            update(t, v)

            @pl.when(t < DEGREE - 1)
            def _():
                hand_out(t + 1, v)
        return carry

    lax.fori_loop(0, DEGREE, step, 0)
    for v in range(V):
        out_ref[v * rows : (v + 1) * rows, :] = cur[v]
    sent_late(DEGREE - 1)


def vmem_limit(least, *sizes):
    return int(min(60 * 2**20, max(least, sum(sizes) + 4 * 2**20)))


def local(vectors, blocks, slot_block_rows, slot_block_columns, counts):
    width, piece = vectors.shape
    slots, size = blocks.shape[2], blocks.shape[3]
    R, C = lax.axis_size("row"), lax.axis_size("col")
    G = R // C
    slab = C * piece
    rows = width // BATCHES
    positions = (slab // size) ** 2 * G
    chunks = next(n for n in (8, 4, 2, 1) if slots % n == 0)
    bf16, f32 = jnp.bfloat16, jnp.float32
    smem, vmem = pl.BlockSpec(memory_space=pltpu.SMEM), pl.BlockSpec(memory_space=pltpu.VMEM)
    hbm = pl.BlockSpec(memory_space=pltpu.HBM)
    dense_shape = (G, slab, slab)
    dense = pl.pallas_call(
        functools.partial(densify_kernel, R, C, chunks),
        out_shape=jax.ShapeDtypeStruct(dense_shape, bf16),
        in_specs=[smem, smem, smem, hbm],
        out_specs=vmem,
        scratch_shapes=[pltpu.VMEM((slots, size, size), bf16)]
        + [pltpu.VMEM((positions + 1, size // PARTS, size), f32)] * PARTS
        + [pltpu.SemaphoreType.DMA((chunks,))],
        compiler_params=pltpu.CompilerParams(vmem_limit_bytes=vmem_limit(51 * 2**20, 2 * slots * size**2, 4 * positions * size**2, 2 * G * slab**2)),
    )(slot_block_rows, slot_block_columns, counts, blocks)

    def dma(*shape):
        return pltpu.SemaphoreType.DMA((DEGREE, BATCHES) + shape)

    def pieces(*shape):
        return pltpu.VMEM((DEGREE, BATCHES) + shape + (rows, piece), bf16)

    return pl.pallas_call(
        functools.partial(filter_kernel, R, C),
        out_shape=jax.ShapeDtypeStruct((width, piece), f32),
        in_specs=[vmem, vmem],
        out_specs=vmem,
        scratch_shapes=[
            pltpu.VMEM(dense_shape, bf16),
            pltpu.VMEM((BATCHES, rows, piece), f32),
            pltpu.VMEM((BATCHES, rows, piece), f32),
            pltpu.VMEM((BATCHES, rows, piece), f32),
            pltpu.VMEM((BATCHES, rows, slab), f32),
            pieces(),
            pieces(C),
            pieces(G, C),
            pieces(C),
            pieces(G, C),
            pieces(C),
            pieces(R),
            dma(C),
            dma(C),
            dma(R),
            dma(G, C),
            dma(C),
            dma(C),
            dma(G, C),
            dma(R),
        ],
        compiler_params=pltpu.CompilerParams(
            collective_id=0, has_side_effects=True, vmem_limit_bytes=vmem_limit(16 * 2**20, 4 * G * slab**2, 12 * DEGREE * (R + C) * width * piece)
        ),
    )(vectors, dense)


def solution(mesh):
    in_specs = (
        P(None, ("row", "col")),
        P("row", "col", None, None, None),
        P("row", "col", None),
        P("row", "col", None),
        P("row", "col"),
    )
    out_specs = P(None, ("row", "col"))
    return jax.shard_map(local, mesh=mesh, in_specs=in_specs, out_specs=out_specs, check_vma=False)
```

```python
import functools

import jax
import jax.numpy as jnp
from jax import lax
from jax.experimental import pallas as pl
from jax.experimental.pallas import tpu as pltpu
from jax.sharding import PartitionSpec as P

DEGREE = 3
CENTER = 0.25
HALF_WIDTH = 2.0
PARTS = 4
BATCHES = 1
MESH = pl.DeviceIdType.MESH


def filter_kernel(
    R, C, chunks, x_ref, rows_ref, cols_ref, count_ref, blocks_ref, out_ref, dense, cur, prev, total, racc, wsend, xrow, xcol, rsend, csend,
    rterm, cterm, xr_s, xr_r, xc_s, xc_r, rt_s, rt_r, ct_s, ct_r,
    rows_v, cols_v, in_s, buf, block_s, before_v, last_v, before_ref, last_ref, chain_s, *sums,
):
    G = R // C
    piece = x_ref.shape[1]
    V, rows = cur.shape[:2]
    a, b = lax.axis_index("row"), lax.axis_index("col")
    my_group, my_col = a // C, a % C

    def alive(j):
        return j + C * (G - 1) >= a

    def above(h):
        return b + C * h > a

    live = alive(b)
    diag = my_col == b

    slots, size = buf.shape[:2]
    per_chunk, slab_blocks, band = slots // chunks, dense.shape[1] // size, size // PARTS

    def chunk_copy(k):
        span = pl.ds(k * per_chunk, per_chunk)
        return pltpu.make_async_copy(blocks_ref.at[0, 0, span], buf.at[span], block_s.at[k])

    def slot_copies():
        return (
            pltpu.make_async_copy(rows_ref, rows_v, in_s.at[0]),
            pltpu.make_async_copy(cols_ref, cols_v, in_s.at[1]),
        )

    def vector_copy(v):
        return pltpu.make_async_copy(x_ref.at[pl.ds(v * rows, rows)], cur.at[v], in_s.at[2 + v])

    @pl.when(live)
    def _():
        for copy in slot_copies():
            copy.start()

    for v in range(V):
        vector_copy(v).start()

    @pl.when(live)
    def _():
        for k in range(chunks):
            chunk_copy(k).start()

    def link_slots():
        positions = last_v.shape[1]
        r, c = rows_v[0], cols_v[0]
        ids = lax.broadcasted_iota(jnp.int32, (1, slots), 1)
        global_row = a * slab_blocks + r
        global_col = (b + C * lax.div(c, slab_blocks)) * slab_blocks + lax.rem(c, slab_blocks)
        used = (ids < count_ref[0, 0]) & (global_row <= global_col)
        key = jnp.where(used, r * (G * slab_blocks) + c, positions)
        down = lax.broadcasted_iota(jnp.int32, (slots, slots), 0)
        across = lax.broadcasted_iota(jnp.int32, (slots, slots), 1)
        keys = jnp.broadcast_to(key, (slots, slots))
        column = jnp.max(jnp.where(down == across, keys, 0), axis=1, keepdims=True)
        before_v[...] = jnp.max(
            jnp.where((column == keys) & (down < across), down + 1, 0), axis=0, keepdims=True
        )
        place = lax.broadcasted_iota(jnp.int32, (slots, positions), 1)
        order = lax.broadcasted_iota(jnp.int32, (slots, positions), 0)
        last_v[...] = jnp.max(jnp.where(column == place, order + 1, 0), axis=0, keepdims=True)

    def chain_copies():
        return (
            pltpu.make_async_copy(before_v, before_ref, chain_s.at[0]),
            pltpu.make_async_copy(last_v, last_ref, chain_s.at[1]),
        )

    barrier = pltpu.get_barrier_semaphore()

    def greet(row, col):
        pl.semaphore_signal(barrier, inc=1, device_id=(row, col), device_id_type=MESH)

    for j in range(C):
        @pl.when(j != b)
        def _():
            greet(a, j)
    for i in range(R - 1):
        @pl.when(i < a)
        def _():
            greet(i, my_col)
    greeted = C - 1 + a
    for h in range(G):
        @pl.when(above(h))
        def _():
            for j in range(C):
                greet(b + C * h, j)
        greeted = greeted + jnp.where(above(h), C, 0)

    @pl.when(live)
    def _():
        for copy in slot_copies():
            copy.wait()
        link_slots()
        for copy in chain_copies():
            copy.start()

    pl.semaphore_wait(barrier, greeted)

    def remote(src, dst, send, recv, row, col):
        return pltpu.make_async_remote_copy(
            src_ref=src, dst_ref=dst, send_sem=send, recv_sem=recv, device_id=(row, col), device_id_type=MESH
        )

    def send_x_col(t, v, i):
        return remote(
            wsend.at[t, v], xcol.at[t, v, my_group, b], xc_s.at[t, v, i], xc_r.at[t, v, my_group, b], i, my_col
        )

    def send_x_row(t, v, j):
        return remote(wsend.at[t, v], xrow.at[t, v, b], xr_s.at[t, v, j], xr_r.at[t, v, b], a, j)

    def send_col_term(t, v, h, j):
        return remote(
            csend.at[t, v, h, j], cterm.at[t, v, a], ct_s.at[t, v, h, j], ct_r.at[t, v, a], b + C * h, j
        )

    def send_row_term(t, v, j):
        return remote(rsend.at[t, v, j], rterm.at[t, v, b], rt_s.at[t, v, j], rt_r.at[t, v, b], a, j)

    def got_x_col(t, v, h, j):
        remote(
            wsend.at[t, v], xcol.at[t, v, h, j], xc_s.at[t, v, 0], xc_r.at[t, v, h, j], b + C * h, j
        ).wait_recv()

    def got_x_row(t, v, j):
        remote(wsend.at[t, v], xrow.at[t, v, j], xr_s.at[t, v, j], xr_r.at[t, v, j], a, j).wait_recv()

    def got_col_term(t, v, i):
        remote(
            csend.at[t, v, 0, 0], cterm.at[t, v, i], ct_s.at[t, v, 0, 0], ct_r.at[t, v, i], i, my_col
        ).wait_recv()

    def got_row_term(t, v, j):
        remote(rsend.at[t, v, j], rterm.at[t, v, j], rt_s.at[t, v, j], rt_r.at[t, v, j], a, j).wait_recv()

    def times(x, m):
        return lax.dot_general(x, m, (((1,), (0,)), ((), ())), preferred_element_type=jnp.float32)

    def times_t(x, m):
        return lax.dot_general(x, m, (((1,), (1,)), ((), ())), preferred_element_type=jnp.float32)

    def densify():
        for copy in chain_copies():
            copy.wait()
        for part in sums:
            part[0] = jnp.zeros(part.shape[1:], part.dtype)

        def chunk(k, carry):
            chunk_copy(k).wait()
            for n in range(per_chunk):
                s = k * per_chunk + n
                before = before_ref[0, s]
                for q, part in enumerate(sums):
                    part[s + 1] = part[before] + buf[s, q * band : (q + 1) * band, :].astype(jnp.float32)
            return carry

        lax.fori_loop(0, chunks, chunk, 0)

        def store(n, carry):
            h, r = n // slab_blocks, n % slab_blocks
            for l in range(slab_blocks):
                last = last_ref[0, (r * G + h) * slab_blocks + l]
                for q, part in enumerate(sums):
                    start = pl.multiple_of(r * size + q * band, band)
                    dense[h, pl.ds(start, band), l * size : (l + 1) * size] = part[last].astype(jnp.bfloat16)
            return carry

        lax.fori_loop(0, G * slab_blocks, store, 0)

    def side_by_side(ref, *index):
        return jnp.concatenate([ref[index + (j,)] for j in range(C)], axis=1)

    def hand_out(t, v):
        w = cur[v].astype(jnp.bfloat16)
        wsend[t, v] = w
        for j in range(C):
            @pl.when((j != b) & alive(j))
            def _():
                send_x_row(t, v, j).start()
        for i in range(R - 1):
            @pl.when(i < a)
            def _():
                send_x_col(t, v, i).start()

        @pl.when(live)
        def _():
            xrow[t, v, b] = w

    def column_terms(t, v):
        for j in range(C):
            @pl.when(j != b)
            def _():
                got_x_row(t, v, j)
        xr = side_by_side(xrow, t, v)
        for h in range(G - 1, -1, -1):
            @pl.when(above(h))
            def _():
                terms = times(xr, dense[h]).astype(jnp.bfloat16)
                for j in range(C):
                    csend[t, v, h, j] = terms[:, j * piece : (j + 1) * piece]
                    send_col_term(t, v, h, j).start()

    def diagonal_terms(t, v):
        @pl.when(diag)
        def _():
            xr = side_by_side(xrow, t, v)
            racc[v] = times(xr, dense[my_group]) + times_t(xr, dense[my_group])

        @pl.when(jnp.logical_not(diag))
        def _():
            racc[v] = jnp.zeros(racc.shape[1:], racc.dtype)

    def row_terms(t, v):
        for h in range(G):
            @pl.when(above(h))
            def _():
                for j in range(C):
                    got_x_col(t, v, h, j)
                racc[v] += times_t(side_by_side(xcol, t, v, h), dense[h])
        for j in range(C):
            mine = racc[v, :, j * piece : (j + 1) * piece].astype(jnp.bfloat16)

            @pl.when(j != b)
            def _():
                rsend[t, v, j] = mine
                send_row_term(t, v, j).start()

            @pl.when(j == b)
            def _():
                rterm[t, v, j] = mine

    def update(t, v):
        total[v] = -CENTER * cur[v]
        for j in range(C):
            @pl.when(alive(j))
            def _():
                @pl.when(j != b)
                def _():
                    got_row_term(t, v, j)
                total[v] += rterm[t, v, j].astype(jnp.float32)
        for i in range(R - 1):
            @pl.when(i < a)
            def _():
                got_col_term(t, v, i)
                total[v] += cterm[t, v, i].astype(jnp.float32)
        scale = jnp.where(t == 0, 1.0 / HALF_WIDTH, 2.0 / HALF_WIDTH)
        following = scale * total[v] - prev[v]
        prev[v] = cur[v]
        cur[v] = following

    for v in range(V):
        vector_copy(v).wait()
        hand_out(0, v)
    prev[...] = jnp.zeros_like(prev)

    @pl.when(live)
    def _():
        densify()

    def sent_early(t):
        for v in range(V):
            for j in range(C):
                @pl.when((j != b) & alive(j))
                def _():
                    send_x_row(t, v, j).wait_send()
            for i in range(R - 1):
                @pl.when(i < a)
                def _():
                    send_x_col(t, v, i).wait_send()
            for h in range(G):
                @pl.when(above(h))
                def _():
                    for j in range(C):
                        send_col_term(t, v, h, j).wait_send()

    def sent_late(t):
        @pl.when(live)
        def _():
            for v in range(V):
                for j in range(C):
                    @pl.when(j != b)
                    def _():
                        send_row_term(t, v, j).wait_send()

    def step(t, carry):
        @pl.when(live)
        def _():
            for v in range(V):
                column_terms(t, v)

            for v in range(V):
                diagonal_terms(t, v)
            for v in range(V):
                row_terms(t, v)
        sent_early(t)

        @pl.when(t > 0)
        def _():
            sent_late(t - 1)

        for v in range(V):
            update(t, v)

            @pl.when(t < DEGREE - 1)
            def _():
                hand_out(t + 1, v)
        return carry

    lax.fori_loop(0, DEGREE, step, 0)
    for v in range(V):
        out_ref[v * rows : (v + 1) * rows, :] = cur[v]
    sent_late(DEGREE - 1)


def vmem_limit(least, *sizes):
    return int(min(60 * 2**20, max(least, sum(sizes) + 4 * 2**20)))


def local(vectors, blocks, slot_block_rows, slot_block_columns, counts):
    width, piece = vectors.shape
    slots, size = blocks.shape[2], blocks.shape[3]
    R, C = lax.axis_size("row"), lax.axis_size("col")
    G = R // C
    slab = C * piece
    rows = width // BATCHES
    positions = (slab // size) ** 2 * G
    chunks = next(n for n in (8, 4, 2, 1) if slots % n == 0)
    bf16, f32 = jnp.bfloat16, jnp.float32
    smem, vmem = pl.BlockSpec(memory_space=pltpu.SMEM), pl.BlockSpec(memory_space=pltpu.VMEM)
    hbm = pl.BlockSpec(memory_space=pltpu.HBM)

    def dma(*shape):
        return pltpu.SemaphoreType.DMA((DEGREE, BATCHES) + shape)

    def pieces(*shape):
        return pltpu.VMEM((DEGREE, BATCHES) + shape + (rows, piece), bf16)

    return pl.pallas_call(
        functools.partial(filter_kernel, R, C, chunks),
        out_shape=jax.ShapeDtypeStruct((width, piece), f32),
        in_specs=[hbm, hbm, hbm, smem, hbm],
        out_specs=vmem,
        scratch_shapes=[
            pltpu.VMEM((G, slab, slab), bf16),
            pltpu.VMEM((BATCHES, rows, piece), f32),
            pltpu.VMEM((BATCHES, rows, piece), f32),
            pltpu.VMEM((BATCHES, rows, piece), f32),
            pltpu.VMEM((BATCHES, rows, slab), f32),
            pieces(),
            pieces(C),
            pieces(G, C),
            pieces(C),
            pieces(G, C),
            pieces(C),
            pieces(R),
            dma(C),
            dma(C),
            dma(R),
            dma(G, C),
            dma(C),
            dma(C),
            dma(G, C),
            dma(R),
            pltpu.VMEM((1, 1, slots), jnp.int32),
            pltpu.VMEM((1, 1, slots), jnp.int32),
            pltpu.SemaphoreType.DMA((2 + BATCHES,)),
            pltpu.VMEM((slots, size, size), bf16),
            pltpu.SemaphoreType.DMA((chunks,)),
            pltpu.VMEM((1, slots), jnp.int32),
            pltpu.VMEM((1, positions), jnp.int32),
            pltpu.SMEM((1, slots), jnp.int32),
            pltpu.SMEM((1, positions), jnp.int32),
            pltpu.SemaphoreType.DMA((2,)),
        ]
        + [pltpu.VMEM((slots + 1, size // PARTS, size), f32)] * PARTS,
        compiler_params=pltpu.CompilerParams(
            collective_id=0, has_side_effects=True, vmem_limit_bytes=vmem_limit(60 * 2**20, 6 * slots * size**2, 2 * G * slab**2, 12 * DEGREE * (R + C) * width * piece)
        ),
    )(vectors, slot_block_rows, slot_block_columns, counts, blocks)


def solution(mesh):
    in_specs = (
        P(None, ("row", "col")),
        P("row", "col", None, None, None),
        P("row", "col", None),
        P("row", "col", None),
        P("row", "col"),
    )
    out_specs = P(None, ("row", "col"))
    return jax.shard_map(local, mesh=mesh, in_specs=in_specs, out_specs=out_specs, check_vma=False)
```

```python
import functools

import jax
import jax.numpy as jnp
from jax import lax
from jax.experimental import pallas as pl
from jax.experimental.pallas import tpu as pltpu
from jax.sharding import PartitionSpec as P

DEGREE = 3
CENTER = 0.25
HALF_WIDTH = 2.0
PARTS = 4
BATCHES = 1
MESH = pl.DeviceIdType.MESH


def filter_kernel(
    R, C, chunks, x_ref, rows_ref, cols_ref, count_ref, blocks_ref, out_ref, dense, cur, prev, total, racc, wsend, xrow, xcol, rsend, csend,
    rterm, cterm, xr_s, xr_r, xc_s, xc_r, rt_s, rt_r, ct_s, ct_r,
    rows_v, cols_v, in_s, buf, block_s, before_v, last_v, before_ref, last_ref, chain_s, *sums,
):
    G = R // C
    piece = x_ref.shape[1]
    V, rows = cur.shape[:2]
    a, b = lax.axis_index("row"), lax.axis_index("col")
    my_group, my_col = a // C, a % C

    def alive(j):
        return j + C * (G - 1) >= a

    def above(h):
        return b + C * h > a

    live = alive(b)
    diag = my_col == b

    slots, size = buf.shape[:2]
    per_chunk, slab_blocks, band = slots // chunks, dense.shape[1] // size, size // PARTS

    def chunk_copy(k):
        span = pl.ds(k * per_chunk, per_chunk)
        return pltpu.make_async_copy(blocks_ref.at[0, 0, span], buf.at[span], block_s.at[k])

    def slot_copies():
        return (
            pltpu.make_async_copy(rows_ref, rows_v, in_s.at[0]),
            pltpu.make_async_copy(cols_ref, cols_v, in_s.at[1]),
        )

    def vector_copy(v):
        return pltpu.make_async_copy(x_ref.at[pl.ds(v * rows, rows)], cur.at[v], in_s.at[2 + v])

    @pl.when(live)
    def _():
        for copy in slot_copies():
            copy.start()

    for v in range(V):
        vector_copy(v).start()

    @pl.when(live)
    def _():
        for k in range(chunks):
            chunk_copy(k).start()

    def link_slots():
        positions = last_v.shape[1]
        r, c = rows_v[0], cols_v[0]
        ids = lax.broadcasted_iota(jnp.int32, (1, slots), 1)
        global_row = a * slab_blocks + r
        global_col = (b + C * lax.div(c, slab_blocks)) * slab_blocks + lax.rem(c, slab_blocks)
        used = (ids < count_ref[0, 0]) & (global_row <= global_col)
        key = jnp.where(used, r * (G * slab_blocks) + c, positions)
        down = lax.broadcasted_iota(jnp.int32, (slots, slots), 0)
        across = lax.broadcasted_iota(jnp.int32, (slots, slots), 1)
        keys = jnp.broadcast_to(key, (slots, slots))
        column = jnp.max(jnp.where(down == across, keys, 0), axis=1, keepdims=True)
        before_v[...] = jnp.max(
            jnp.where((column == keys) & (down < across), down + 1, 0), axis=0, keepdims=True
        )
        place = lax.broadcasted_iota(jnp.int32, (slots, positions), 1)
        order = lax.broadcasted_iota(jnp.int32, (slots, positions), 0)
        last_v[...] = jnp.max(jnp.where(column == place, order + 1, 0), axis=0, keepdims=True)

    def chain_copies():
        return (
            pltpu.make_async_copy(before_v, before_ref, chain_s.at[0]),
            pltpu.make_async_copy(last_v, last_ref, chain_s.at[1]),
        )

    def add_chunks(first, end):
        def chunk(k, carry):
            chunk_copy(k).wait()
            for n in range(per_chunk):
                s = k * per_chunk + n
                before = before_ref[0, s]
                for q, part in enumerate(sums):
                    part[s + 1] = part[before] + buf[s, q * band : (q + 1) * band, :].astype(jnp.float32)
            return carry

        lax.fori_loop(first, end, chunk, 0)

    def begin_dense():
        for copy in slot_copies():
            copy.wait()
        link_slots()
        for copy in chain_copies():
            copy.start()
        for part in sums:
            part[0] = jnp.zeros(part.shape[1:], part.dtype)
        for copy in chain_copies():
            copy.wait()
        add_chunks(0, chunks * 3 // 8)

    def finish_dense():
        add_chunks(chunks * 3 // 8, chunks)

        def store(n, carry):
            h, r = n // slab_blocks, n % slab_blocks
            for l in range(slab_blocks):
                last = last_ref[0, (r * G + h) * slab_blocks + l]
                for q, part in enumerate(sums):
                    start = pl.multiple_of(r * size + q * band, band)
                    dense[h, pl.ds(start, band), l * size : (l + 1) * size] = part[last].astype(jnp.bfloat16)
            return carry

        lax.fori_loop(0, G * slab_blocks, store, 0)

    barrier = pltpu.get_barrier_semaphore()

    def greet(row, col):
        pl.semaphore_signal(barrier, inc=1, device_id=(row, col), device_id_type=MESH)

    for j in range(C):
        @pl.when(j != b)
        def _():
            greet(a, j)
    for i in range(R - 1):
        @pl.when(i < a)
        def _():
            greet(i, my_col)
    greeted = C - 1 + a
    for h in range(G):
        @pl.when(above(h))
        def _():
            for j in range(C):
                greet(b + C * h, j)
        greeted = greeted + jnp.where(above(h), C, 0)

    @pl.when(live)
    def _():
        begin_dense()

    pl.semaphore_wait(barrier, greeted)

    def remote(src, dst, send, recv, row, col):
        return pltpu.make_async_remote_copy(
            src_ref=src, dst_ref=dst, send_sem=send, recv_sem=recv, device_id=(row, col), device_id_type=MESH
        )

    def send_x_col(t, v, i):
        return remote(
            wsend.at[t, v], xcol.at[t, v, my_group, b], xc_s.at[t, v, i], xc_r.at[t, v, my_group, b], i, my_col
        )

    def send_x_row(t, v, j):
        return remote(wsend.at[t, v], xrow.at[t, v, b], xr_s.at[t, v, j], xr_r.at[t, v, b], a, j)

    def send_col_term(t, v, h, j):
        return remote(
            csend.at[t, v, h, j], cterm.at[t, v, a], ct_s.at[t, v, h, j], ct_r.at[t, v, a], b + C * h, j
        )

    def send_row_term(t, v, j):
        return remote(rsend.at[t, v, j], rterm.at[t, v, b], rt_s.at[t, v, j], rt_r.at[t, v, b], a, j)

    def got_x_col(t, v, h, j):
        remote(
            wsend.at[t, v], xcol.at[t, v, h, j], xc_s.at[t, v, 0], xc_r.at[t, v, h, j], b + C * h, j
        ).wait_recv()

    def got_x_row(t, v, j):
        remote(wsend.at[t, v], xrow.at[t, v, j], xr_s.at[t, v, j], xr_r.at[t, v, j], a, j).wait_recv()

    def got_col_term(t, v, i):
        remote(
            csend.at[t, v, 0, 0], cterm.at[t, v, i], ct_s.at[t, v, 0, 0], ct_r.at[t, v, i], i, my_col
        ).wait_recv()

    def got_row_term(t, v, j):
        remote(rsend.at[t, v, j], rterm.at[t, v, j], rt_s.at[t, v, j], rt_r.at[t, v, j], a, j).wait_recv()

    def times(x, m):
        return lax.dot_general(x, m, (((1,), (0,)), ((), ())), preferred_element_type=jnp.float32)

    def times_t(x, m):
        return lax.dot_general(x, m, (((1,), (1,)), ((), ())), preferred_element_type=jnp.float32)

    def side_by_side(ref, *index):
        return jnp.concatenate([ref[index + (j,)] for j in range(C)], axis=1)

    def hand_out(t, v):
        w = cur[v].astype(jnp.bfloat16)
        wsend[t, v] = w
        for j in range(C):
            @pl.when((j != b) & alive(j))
            def _():
                send_x_row(t, v, j).start()
        for i in range(R - 1):
            @pl.when(i < a)
            def _():
                send_x_col(t, v, i).start()

        @pl.when(live)
        def _():
            xrow[t, v, b] = w

    def column_terms(t, v):
        for j in range(C):
            @pl.when(j != b)
            def _():
                got_x_row(t, v, j)
        xr = side_by_side(xrow, t, v)
        for h in range(G - 1, -1, -1):
            @pl.when(above(h))
            def _():
                terms = times(xr, dense[h]).astype(jnp.bfloat16)
                for j in range(C):
                    csend[t, v, h, j] = terms[:, j * piece : (j + 1) * piece]
                    send_col_term(t, v, h, j).start()

    def diagonal_terms(t, v):
        @pl.when(diag)
        def _():
            xr = side_by_side(xrow, t, v)
            racc[v] = times(xr, dense[my_group]) + times_t(xr, dense[my_group])

        @pl.when(jnp.logical_not(diag))
        def _():
            racc[v] = jnp.zeros(racc.shape[1:], racc.dtype)

    def row_terms(t, v):
        for h in range(G):
            @pl.when(above(h))
            def _():
                for j in range(C):
                    got_x_col(t, v, h, j)
                racc[v] += times_t(side_by_side(xcol, t, v, h), dense[h])
        for j in range(C):
            mine = racc[v, :, j * piece : (j + 1) * piece].astype(jnp.bfloat16)

            @pl.when(j != b)
            def _():
                rsend[t, v, j] = mine
                send_row_term(t, v, j).start()

            @pl.when(j == b)
            def _():
                rterm[t, v, j] = mine

    def update(t, v):
        total[v] = -CENTER * cur[v]
        for j in range(C):
            @pl.when(alive(j))
            def _():
                @pl.when(j != b)
                def _():
                    got_row_term(t, v, j)
                total[v] += rterm[t, v, j].astype(jnp.float32)
        for i in range(R - 1):
            @pl.when(i < a)
            def _():
                got_col_term(t, v, i)
                total[v] += cterm[t, v, i].astype(jnp.float32)
        scale = jnp.where(t == 0, 1.0 / HALF_WIDTH, 2.0 / HALF_WIDTH)
        following = scale * total[v] - prev[v]
        prev[v] = cur[v]
        cur[v] = following

    for v in range(V):
        vector_copy(v).wait()
        hand_out(0, v)
    prev[...] = jnp.zeros_like(prev)

    @pl.when(live)
    def _():
        finish_dense()

    def sent_early(t):
        for v in range(V):
            for j in range(C):
                @pl.when((j != b) & alive(j))
                def _():
                    send_x_row(t, v, j).wait_send()
            for i in range(R - 1):
                @pl.when(i < a)
                def _():
                    send_x_col(t, v, i).wait_send()
            for h in range(G):
                @pl.when(above(h))
                def _():
                    for j in range(C):
                        send_col_term(t, v, h, j).wait_send()

    def sent_late(t):
        @pl.when(live)
        def _():
            for v in range(V):
                for j in range(C):
                    @pl.when(j != b)
                    def _():
                        send_row_term(t, v, j).wait_send()

    def step(t, carry):
        @pl.when(live)
        def _():
            for v in range(V):
                column_terms(t, v)

            for v in range(V):
                diagonal_terms(t, v)
            for v in range(V):
                row_terms(t, v)

        @pl.when(t > 0)
        def _():
            sent_early(t - 1)
            sent_late(t - 1)

        @pl.when(t == DEGREE - 1)
        def _():
            sent_early(t)

        for v in range(V):
            update(t, v)

            @pl.when(t < DEGREE - 1)
            def _():
                hand_out(t + 1, v)
        return carry

    lax.fori_loop(0, DEGREE, step, 0)
    for v in range(V):
        out_ref[v * rows : (v + 1) * rows, :] = cur[v]
    sent_late(DEGREE - 1)


def vmem_limit(least, *sizes):
    return int(min(60 * 2**20, max(least, sum(sizes) + 4 * 2**20)))


def local(vectors, blocks, slot_block_rows, slot_block_columns, counts):
    width, piece = vectors.shape
    slots, size = blocks.shape[2], blocks.shape[3]
    R, C = lax.axis_size("row"), lax.axis_size("col")
    G = R // C
    slab = C * piece
    rows = width // BATCHES
    positions = (slab // size) ** 2 * G
    chunks = next(n for n in (8, 4, 2, 1) if slots % n == 0)
    bf16, f32 = jnp.bfloat16, jnp.float32
    smem, vmem = pl.BlockSpec(memory_space=pltpu.SMEM), pl.BlockSpec(memory_space=pltpu.VMEM)
    hbm = pl.BlockSpec(memory_space=pltpu.HBM)

    def dma(*shape):
        return pltpu.SemaphoreType.DMA((DEGREE, BATCHES) + shape)

    def pieces(*shape):
        return pltpu.VMEM((DEGREE, BATCHES) + shape + (rows, piece), bf16)

    return pl.pallas_call(
        functools.partial(filter_kernel, R, C, chunks),
        out_shape=jax.ShapeDtypeStruct((width, piece), f32),
        in_specs=[hbm, hbm, hbm, smem, hbm],
        out_specs=vmem,
        scratch_shapes=[
            pltpu.VMEM((G, slab, slab), bf16),
            pltpu.VMEM((BATCHES, rows, piece), f32),
            pltpu.VMEM((BATCHES, rows, piece), f32),
            pltpu.VMEM((BATCHES, rows, piece), f32),
            pltpu.VMEM((BATCHES, rows, slab), f32),
            pieces(),
            pieces(C),
            pieces(G, C),
            pieces(C),
            pieces(G, C),
            pieces(C),
            pieces(R),
            dma(C),
            dma(C),
            dma(R),
            dma(G, C),
            dma(C),
            dma(C),
            dma(G, C),
            dma(R),
            pltpu.VMEM((1, 1, slots), jnp.int32),
            pltpu.VMEM((1, 1, slots), jnp.int32),
            pltpu.SemaphoreType.DMA((2 + BATCHES,)),
            pltpu.VMEM((slots, size, size), bf16),
            pltpu.SemaphoreType.DMA((chunks,)),
            pltpu.VMEM((1, slots), jnp.int32),
            pltpu.VMEM((1, positions), jnp.int32),
            pltpu.SMEM((1, slots), jnp.int32),
            pltpu.SMEM((1, positions), jnp.int32),
            pltpu.SemaphoreType.DMA((2,)),
        ]
        + [pltpu.VMEM((slots + 1, size // PARTS, size), f32)] * PARTS,
        compiler_params=pltpu.CompilerParams(
            collective_id=0, has_side_effects=True, vmem_limit_bytes=vmem_limit(60 * 2**20, 6 * slots * size**2, 2 * G * slab**2, 12 * DEGREE * (R + C) * width * piece)
        ),
    )(vectors, slot_block_rows, slot_block_columns, counts, blocks)


def solution(mesh):
    in_specs = (
        P(None, ("row", "col")),
        P("row", "col", None, None, None),
        P("row", "col", None),
        P("row", "col", None),
        P("row", "col"),
    )
    out_specs = P(None, ("row", "col"))
    return jax.shard_map(local, mesh=mesh, in_specs=in_specs, out_specs=out_specs, check_vma=False)
```

```python
import functools

import jax
import jax.numpy as jnp
from jax import lax
from jax.experimental import pallas as pl
from jax.experimental.pallas import tpu as pltpu
from jax.sharding import PartitionSpec as P

DEGREE = 3
CENTER = 0.25
HALF_WIDTH = 2.0
PARTS = 4
BATCHES = 1
MESH = pl.DeviceIdType.MESH


def filter_kernel(
    R, C, chunks, x_ref, rows_ref, cols_ref, count_ref, blocks_ref, out_ref, dense, cur, prev, total, racc, wsend, xrow, xcol, rsend, csend,
    rterm, cterm, xr_s, xr_r, xc_s, xc_r, rt_s, rt_r, ct_s, ct_r,
    rows_v, cols_v, in_s, buf, block_s, before_v, last_v, before_ref, last_ref, chain_s, *sums,
):
    G = R // C
    piece = x_ref.shape[1]
    V, rows = cur.shape[:2]
    a, b = lax.axis_index("row"), lax.axis_index("col")
    my_group, my_col = a // C, a % C

    def alive(j):
        return j + C * (G - 1) >= a

    def above(h):
        return b + C * h > a

    live = alive(b)
    diag = my_col == b

    slots, size = buf.shape[:2]
    per_chunk, slab_blocks, band = slots // chunks, dense.shape[1] // size, size // PARTS

    def chunk_copy(k):
        span = pl.ds(k * per_chunk, per_chunk)
        return pltpu.make_async_copy(blocks_ref.at[0, 0, span], buf.at[span], block_s.at[k])

    def slot_copies():
        return (
            pltpu.make_async_copy(rows_ref, rows_v, in_s.at[0]),
            pltpu.make_async_copy(cols_ref, cols_v, in_s.at[1]),
        )

    def vector_copy(v):
        return pltpu.make_async_copy(x_ref.at[pl.ds(v * rows, rows)], cur.at[v], in_s.at[2 + v])

    @pl.when(live)
    def _():
        for copy in slot_copies():
            copy.start()

    for v in range(V):
        vector_copy(v).start()

    @pl.when(live)
    def _():
        for k in range(chunks):
            chunk_copy(k).start()

    def link_slots():
        positions = last_v.shape[1]
        r, c = rows_v[0], cols_v[0]
        ids = lax.broadcasted_iota(jnp.int32, (1, slots), 1)
        global_row = a * slab_blocks + r
        global_col = (b + C * lax.div(c, slab_blocks)) * slab_blocks + lax.rem(c, slab_blocks)
        used = (ids < count_ref[0, 0]) & (global_row <= global_col)
        key = jnp.where(used, r * (G * slab_blocks) + c, positions)
        down = lax.broadcasted_iota(jnp.int32, (slots, slots), 0)
        across = lax.broadcasted_iota(jnp.int32, (slots, slots), 1)
        keys = jnp.broadcast_to(key, (slots, slots))
        column = jnp.max(jnp.where(down == across, keys, 0), axis=1, keepdims=True)
        before_v[...] = jnp.max(
            jnp.where((column == keys) & (down < across), down + 1, 0), axis=0, keepdims=True
        )
        place = lax.broadcasted_iota(jnp.int32, (slots, positions), 1)
        order = lax.broadcasted_iota(jnp.int32, (slots, positions), 0)
        last_v[...] = jnp.max(jnp.where(column == place, order + 1, 0), axis=0, keepdims=True)

    def chain_copies():
        return (
            pltpu.make_async_copy(before_v, before_ref, chain_s.at[0]),
            pltpu.make_async_copy(last_v, last_ref, chain_s.at[1]),
        )

    barrier = pltpu.get_barrier_semaphore()

    def greet(row, col):
        pl.semaphore_signal(barrier, inc=1, device_id=(row, col), device_id_type=MESH)

    for j in range(C):
        @pl.when(j != b)
        def _():
            greet(a, j)
    for i in range(R - 1):
        @pl.when(i < a)
        def _():
            greet(i, my_col)
    greeted = C - 1 + a
    for h in range(G):
        @pl.when(above(h))
        def _():
            for j in range(C):
                greet(b + C * h, j)
        greeted = greeted + jnp.where(above(h), C, 0)

    @pl.when(live)
    def _():
        for copy in slot_copies():
            copy.wait()
        link_slots()
        for copy in chain_copies():
            copy.start()

    pl.semaphore_wait(barrier, greeted)

    def remote(src, dst, send, recv, row, col):
        return pltpu.make_async_remote_copy(
            src_ref=src, dst_ref=dst, send_sem=send, recv_sem=recv, device_id=(row, col), device_id_type=MESH
        )

    def send_x_col(t, v, i):
        return remote(
            wsend.at[t, v], xcol.at[t, v, my_group, b], xc_s.at[t, v, i], xc_r.at[t, v, my_group, b], i, my_col
        )

    def send_x_row(t, v, j):
        return remote(wsend.at[t, v], xrow.at[t, v, b], xr_s.at[t, v, j], xr_r.at[t, v, b], a, j)

    def send_col_term(t, v, h, j):
        return remote(
            csend.at[t, v, h, j], cterm.at[t, v, a], ct_s.at[t, v, h, j], ct_r.at[t, v, a], b + C * h, j
        )

    def send_row_term(t, v, j):
        return remote(rsend.at[t, v, j], rterm.at[t, v, b], rt_s.at[t, v, j], rt_r.at[t, v, b], a, j)

    def got_x_col(t, v, h, j):
        remote(
            wsend.at[t, v], xcol.at[t, v, h, j], xc_s.at[t, v, 0], xc_r.at[t, v, h, j], b + C * h, j
        ).wait_recv()

    def got_x_row(t, v, j):
        remote(wsend.at[t, v], xrow.at[t, v, j], xr_s.at[t, v, j], xr_r.at[t, v, j], a, j).wait_recv()

    def got_col_term(t, v, i):
        remote(
            csend.at[t, v, 0, 0], cterm.at[t, v, i], ct_s.at[t, v, 0, 0], ct_r.at[t, v, i], i, my_col
        ).wait_recv()

    def got_row_term(t, v, j):
        remote(rsend.at[t, v, j], rterm.at[t, v, j], rt_s.at[t, v, j], rt_r.at[t, v, j], a, j).wait_recv()

    def times(x, m):
        return lax.dot_general(x, m, (((1,), (0,)), ((), ())), preferred_element_type=jnp.float32)

    def times_t(x, m):
        return lax.dot_general(x, m, (((1,), (1,)), ((), ())), preferred_element_type=jnp.float32)

    def densify():
        for copy in chain_copies():
            copy.wait()
        for part in sums:
            part[0] = jnp.zeros(part.shape[1:], part.dtype)

        def chunk(k, carry):
            chunk_copy(k).wait()
            for n in range(per_chunk):
                s = k * per_chunk + n
                before = before_ref[0, s]
                for q, part in enumerate(sums):
                    part[s + 1] = part[before] + buf[s, q * band : (q + 1) * band, :].astype(jnp.float32)
            return carry

        lax.fori_loop(0, chunks, chunk, 0)

        def store(n, carry):
            h, r = n // slab_blocks, n % slab_blocks
            for l in range(slab_blocks):
                last = last_ref[0, (r * G + h) * slab_blocks + l]
                for q, part in enumerate(sums):
                    start = pl.multiple_of(r * size + q * band, band)
                    dense[h, pl.ds(start, band), l * size : (l + 1) * size] = part[last].astype(jnp.bfloat16)
            return carry

        lax.fori_loop(0, G * slab_blocks, store, 0)

    def side_by_side(ref, *index):
        return jnp.concatenate([ref[index + (j,)] for j in range(C)], axis=1)

    def hand_out(t, v):
        w = cur[v].astype(jnp.bfloat16)
        wsend[t, v] = w
        for i in range(R - 1):
            @pl.when(i < a)
            def _():
                send_x_col(t, v, i).start()
        for j in range(C):
            @pl.when((j != b) & alive(j))
            def _():
                send_x_row(t, v, j).start()

        @pl.when(live)
        def _():
            xrow[t, v, b] = w

    def column_terms(t, v):
        for j in range(C):
            @pl.when(j != b)
            def _():
                got_x_row(t, v, j)
        xr = side_by_side(xrow, t, v)
        for h in range(G - 1, -1, -1):
            @pl.when(above(h))
            def _():
                terms = times(xr, dense[h]).astype(jnp.bfloat16)
                for j in range(C):
                    csend[t, v, h, j] = terms[:, j * piece : (j + 1) * piece]
                    send_col_term(t, v, h, j).start()

    def diagonal_terms(t, v):
        @pl.when(diag)
        def _():
            xr = side_by_side(xrow, t, v)
            racc[v] = times(xr, dense[my_group]) + times_t(xr, dense[my_group])

        @pl.when(jnp.logical_not(diag))
        def _():
            racc[v] = jnp.zeros(racc.shape[1:], racc.dtype)

    def row_terms(t, v):
        for h in range(G):
            @pl.when(above(h))
            def _():
                for j in range(C):
                    got_x_col(t, v, h, j)
                racc[v] += times_t(side_by_side(xcol, t, v, h), dense[h])
        for j in range(C):
            mine = racc[v, :, j * piece : (j + 1) * piece].astype(jnp.bfloat16)

            @pl.when(j != b)
            def _():
                rsend[t, v, j] = mine
                send_row_term(t, v, j).start()

            @pl.when(j == b)
            def _():
                rterm[t, v, j] = mine

    def update(t, v):
        total[v] = -CENTER * cur[v]
        for j in range(C):
            @pl.when(alive(j))
            def _():
                @pl.when(j != b)
                def _():
                    got_row_term(t, v, j)
                total[v] += rterm[t, v, j].astype(jnp.float32)
        for i in range(R - 1):
            @pl.when(i < a)
            def _():
                got_col_term(t, v, i)
                total[v] += cterm[t, v, i].astype(jnp.float32)
        scale = jnp.where(t == 0, 1.0 / HALF_WIDTH, 2.0 / HALF_WIDTH)
        following = scale * total[v] - prev[v]
        prev[v] = cur[v]
        cur[v] = following

    for v in range(V):
        vector_copy(v).wait()
        hand_out(0, v)
    prev[...] = jnp.zeros_like(prev)

    @pl.when(live)
    def _():
        densify()

    def sent_early(t):
        for v in range(V):
            for j in range(C):
                @pl.when((j != b) & alive(j))
                def _():
                    send_x_row(t, v, j).wait_send()
            for i in range(R - 1):
                @pl.when(i < a)
                def _():
                    send_x_col(t, v, i).wait_send()
            for h in range(G):
                @pl.when(above(h))
                def _():
                    for j in range(C):
                        send_col_term(t, v, h, j).wait_send()

    def sent_late(t):
        @pl.when(live)
        def _():
            for v in range(V):
                for j in range(C):
                    @pl.when(j != b)
                    def _():
                        send_row_term(t, v, j).wait_send()

    def step(t, carry):
        @pl.when(live)
        def _():
            for v in range(V):
                column_terms(t, v)

            for v in range(V):
                diagonal_terms(t, v)
            for v in range(V):
                row_terms(t, v)

        @pl.when(t > 0)
        def _():
            sent_early(t - 1)
            sent_late(t - 1)

        @pl.when(t == DEGREE - 1)
        def _():
            sent_early(t)

        for v in range(V):
            update(t, v)

            @pl.when(t < DEGREE - 1)
            def _():
                hand_out(t + 1, v)
        return carry

    lax.fori_loop(0, DEGREE, step, 0)
    for v in range(V):
        out_ref[v * rows : (v + 1) * rows, :] = cur[v]
    sent_late(DEGREE - 1)


def vmem_limit(least, *sizes):
    return int(min(60 * 2**20, max(least, sum(sizes) + 4 * 2**20)))


def local(vectors, blocks, slot_block_rows, slot_block_columns, counts):
    width, piece = vectors.shape
    slots, size = blocks.shape[2], blocks.shape[3]
    R, C = lax.axis_size("row"), lax.axis_size("col")
    G = R // C
    slab = C * piece
    rows = width // BATCHES
    positions = (slab // size) ** 2 * G
    chunks = next(n for n in (8, 4, 2, 1) if slots % n == 0)
    bf16, f32 = jnp.bfloat16, jnp.float32
    smem, vmem = pl.BlockSpec(memory_space=pltpu.SMEM), pl.BlockSpec(memory_space=pltpu.VMEM)
    hbm = pl.BlockSpec(memory_space=pltpu.HBM)

    def dma(*shape):
        return pltpu.SemaphoreType.DMA((DEGREE, BATCHES) + shape)

    def pieces(*shape):
        return pltpu.VMEM((DEGREE, BATCHES) + shape + (rows, piece), bf16)

    return pl.pallas_call(
        functools.partial(filter_kernel, R, C, chunks),
        out_shape=jax.ShapeDtypeStruct((width, piece), f32),
        in_specs=[hbm, hbm, hbm, smem, hbm],
        out_specs=vmem,
        scratch_shapes=[
            pltpu.VMEM((G, slab, slab), bf16),
            pltpu.VMEM((BATCHES, rows, piece), f32),
            pltpu.VMEM((BATCHES, rows, piece), f32),
            pltpu.VMEM((BATCHES, rows, piece), f32),
            pltpu.VMEM((BATCHES, rows, slab), f32),
            pieces(),
            pieces(C),
            pieces(G, C),
            pieces(C),
            pieces(G, C),
            pieces(C),
            pieces(R),
            dma(C),
            dma(C),
            dma(R),
            dma(G, C),
            dma(C),
            dma(C),
            dma(G, C),
            dma(R),
            pltpu.VMEM((1, 1, slots), jnp.int32),
            pltpu.VMEM((1, 1, slots), jnp.int32),
            pltpu.SemaphoreType.DMA((2 + BATCHES,)),
            pltpu.VMEM((slots, size, size), bf16),
            pltpu.SemaphoreType.DMA((chunks,)),
            pltpu.VMEM((1, slots), jnp.int32),
            pltpu.VMEM((1, positions), jnp.int32),
            pltpu.SMEM((1, slots), jnp.int32),
            pltpu.SMEM((1, positions), jnp.int32),
            pltpu.SemaphoreType.DMA((2,)),
        ]
        + [pltpu.VMEM((slots + 1, size // PARTS, size), f32)] * PARTS,
        compiler_params=pltpu.CompilerParams(
            collective_id=0, has_side_effects=True, vmem_limit_bytes=vmem_limit(60 * 2**20, 6 * slots * size**2, 2 * G * slab**2, 12 * DEGREE * (R + C) * width * piece)
        ),
    )(vectors, slot_block_rows, slot_block_columns, counts, blocks)


def solution(mesh):
    in_specs = (
        P(None, ("row", "col")),
        P("row", "col", None, None, None),
        P("row", "col", None),
        P("row", "col", None),
        P("row", "col"),
    )
    out_specs = P(None, ("row", "col"))
    return jax.shard_map(local, mesh=mesh, in_specs=in_specs, out_specs=out_specs, check_vma=False)
```
